32 devices in a mesh: section: 2 (over core), fsdp: 4 (over y, x), rep: 4 (over z).
Axes of the slice: x: 2, y: 2, z: 4, core: 2. Of those that a mesh axis runs over, the one named last changes fastest.
Arguments:
- tokens: bfloat16 [2, 4, 2048, 640], P(None, 'rep', 'fsdp'), may hold values from -6 to 6
- cotangent: bfloat16 [2, 4, 2048, 640], P(None, 'rep', 'fsdp'), may hold values from -6 to 6
- lengths: int32 [2, 4, 4], P(None, 'rep'), may hold values from 1 to 1538, 2048 in all within a row
- query_weight: bfloat16 [2, 640, 1024], P('section', 'fsdp'), may hold values from -0.25 to 0.25
- key_weight: bfloat16 [2, 640, 256], P('section', 'fsdp'), may hold values from -0.25 to 0.25
- value_weight: bfloat16 [2, 640, 256], P('section', 'fsdp'), may hold values from -0.25 to 0.25
- out_weight: bfloat16 [2, 1024, 640], P('section', 'fsdp'), may hold values from -0.1875 to 0.1875
- gate_weight: bfloat16 [2, 640, 2048], P('section', 'fsdp'), may hold values from -0.25 to 0.25
- up_weight: bfloat16 [2, 640, 2048], P('section', 'fsdp'), may hold values from -0.25 to 0.25
- down_weight: bfloat16 [2, 2048, 640], P('section', 'fsdp'), may hold values from -0.125 to 0.125
- norm_gains: bfloat16 [2, 4, 640], P('section', None, 'fsdp'), may hold values from 0.5 to 1.5
- head_gains: bfloat16 [2, 2, 256], P('section', None, 'fsdp'), may hold values from 0.5 to 1.5
Outputs:
- section_out: bfloat16 [2, 2, 4, 2048, 640], P('section', None, 'rep', 'fsdp')
- input_grad: float32 [2, 2, 4, 2048, 640], P('section', None, 'rep', 'fsdp')
- grad_query_weight: float32 [2, 640, 1024], P('section', 'fsdp')
- grad_key_weight: float32 [2, 640, 256], P('section', 'fsdp')
- grad_value_weight: float32 [2, 640, 256], P('section', 'fsdp')
- grad_out_weight: float32 [2, 1024, 640], P('section', 'fsdp')
- grad_gate_weight: float32 [2, 640, 2048], P('section', 'fsdp')
- grad_up_weight: float32 [2, 640, 2048], P('section', 'fsdp')
- grad_down_weight: float32 [2, 2048, 640], P('section', 'fsdp')
- grad_norm_gains: float32 [2, 4, 640], P('section', None, 'fsdp')
- grad_head_gains: float32 [2, 2, 256], P('section', None, 'fsdp')
The draws below stay inside these ranges and needn't reach their ends.
Inputs may be any that keep to these rules, and one draw needn't show every extreme that they name: In each micro-batch and group the 4 lengths sum to exactly 2048, so every group holds the same number of tokens, and the longest is exactly 1538.
All inputs are finite; a program needn't handle non-finite values.
Results may differ from the reference program's by a relative error of at most 0.028.
Values may be sent and summed in bfloat16 or wider, within the bound.
A program may use at most 192 MiB of HBM per device.

```python
import math
import jax
import jax.numpy as jnp
import numpy as np
from jax import lax

D = 640
H = 4
HD = 256
FF = 2048
WINDOW = 512
TOK_DEV = 512
MICRO = 2
NDOC = 4
QW = 1024
TOK_GROUP = 2048
GROUPS = 4


def levels(rng, dims, cuts, low, top_value):
    factor_of = 1.0
    for dim, blocks in cuts:
        steps = jax.random.uniform(jax.random.fold_in(jax.random.fold_in(rng, 6), dim), (blocks,), jnp.float32, low / len(cuts), top_value / len(cuts))
        factor_of = factor_of * jnp.repeat(jnp.exp(steps), dims[dim] // blocks).reshape((-1,) + (1,) * (len(dims) - 1 - dim))
    return factor_of


def length_profile(amount, total, limit, lean):
    portions = [(1 << 20) // math.isqrt(grade ** lean) + 1 for grade in range(2, amount + 1)]
    surplus, given = total - limit - (amount - 1), [1] * (amount - 1)
    while surplus > 0:
        free = [i for i in range(amount - 1) if given[i] < limit]
        pool, left = sum([portions[i] for i in free]), surplus
        for i in free:
            more = min(limit - given[i], max(1, left * portions[i] // pool), surplus)
            given[i] = given[i] + more
            surplus = surplus - more
    return np.array([limit] + given)


def ragged(key, count, total, limit, skew):
    if count == 2:
        one = jax.random.randint(key, (), max(1, total - limit), min(limit, total - 1) + 1)
        return jnp.stack([one, total - one])
    tallies = jnp.asarray(length_profile(count, total, limit, skew), jnp.int32)
    twos = (count - 1) // 2
    donor, receiver = tallies[1:1 + 2 * twos:2], tallies[2:2 + 2 * twos:2]
    margin = jnp.minimum(donor - 1, limit - receiver)
    passed = jax.random.randint(jax.random.fold_in(key, 1), (twos,), 0, 1 << 20) % (margin + 1)
    tallies = tallies.at[1:1 + 2 * twos:2].set(donor - passed).at[2:2 + 2 * twos:2].set(receiver + passed)
    return tallies[jax.random.permutation(jax.random.fold_in(key, 2), count)]


def gaussian(key, dims, spread, bound, pieces=(), held_as=jnp.bfloat16):
    values = jax.random.normal(key, dims, jnp.float32) * spread
    if len(pieces) > 0:
        values = levels(key, dims, pieces, -0.22, 0.18) * values
    return jnp.clip(values, min=-bound, max=bound).astype(held_as)


def setup_inputs(seed: int = 0) -> dict:
    key_list = jax.random.split(jax.random.key(seed), 13)
    return {
        "tokens": gaussian(key_list[0], (MICRO, GROUPS, TOK_GROUP, D), 1.0, 6.0, ((1, 4), (2, 4))),
        "cotangent": gaussian(key_list[1], (MICRO, GROUPS, TOK_GROUP, D), 1.0, 6.0, ((1, 4), (2, 4))),
        "lengths": jax.vmap(lambda own: ragged(own, NDOC, TOK_GROUP, TOK_GROUP - TOK_DEV + 2, 0))(jax.random.split(key_list[2], MICRO * GROUPS)).reshape((MICRO, GROUPS, NDOC)).astype(jnp.int32),
        "query_weight": gaussian(key_list[3], (2, D, QW), D ** -0.5, 0.25, ((0, 2), (1, 4))),
        "key_weight": gaussian(key_list[4], (2, D, HD), D ** -0.5, 0.25, ((0, 2), (1, 4))),
        "value_weight": gaussian(key_list[5], (2, D, HD), D ** -0.5, 0.25, ((0, 2), (1, 4))),
        "out_weight": gaussian(key_list[6], (2, QW, D), QW ** -0.5, 0.1875, ((0, 2), (1, 4))),
        "gate_weight": gaussian(key_list[7], (2, D, FF), D ** -0.5, 0.25, ((0, 2), (1, 4))),
        "up_weight": gaussian(key_list[8], (2, D, FF), D ** -0.5, 0.25, ((0, 2), (1, 4))),
        "down_weight": gaussian(key_list[9], (2, FF, D), FF ** -0.5, 0.125, ((0, 2), (1, 4))),
        "norm_gains": jnp.clip(1.0 + 0.1 * jax.random.normal(key_list[10], (2, 4, D), jnp.float32), 0.5, 1.5).astype(jnp.bfloat16),
        "head_gains": jnp.clip(1.0 + 0.1 * jax.random.normal(key_list[11], (2, 2, HD), jnp.float32), 0.5, 1.5).astype(jnp.bfloat16),
    }


epsilon = 1e-06
rope_base = 10000.0
neg_fill = -1e+30
gelu_coef = 0.7978845608028654

@jax.custom_vjp
def low(v):
    return lax.optimization_barrier(v.astype(jnp.bfloat16)).astype(jnp.float32)

@jax.custom_vjp
def low_back(v):
    return v

def low_keep(v):
    return (low(v), None)

def low_pass(kept, grad):
    return (grad,)

def back_keep(v):
    return (v, None)

def back_low(kept, grad):
    return (low(grad),)
low.defvjp(low_keep, low_pass)
low_back.defvjp(back_keep, back_low)

def exact_dot(left, right):
    return jnp.dot(left, right, precision=lax.Precision.HIGHEST, preferred_element_type=jnp.float32)

def rms_scale(vector, gain_vec):
    return vector * lax.rsqrt(lax.optimization_barrier(jnp.mean(vector * vector, axis=-1, keepdims=True)) + epsilon) * gain_vec

def gelu_tanh(vector):
    return 0.5 * vector * (1.0 + jnp.tanh(gelu_coef * (vector + 0.044715 * vector * vector * vector)))

def rotate(vector, cosine, sine_table):
    half_width = vector.shape[-1] // 2
    first_half = vector[..., :half_width]
    second_half = vector[..., half_width:]
    return jnp.concatenate([first_half * cosine - second_half * sine_table, second_half * cosine + first_half * sine_table], axis=-1)

def angle_tables(offset, width):
    frequency = jnp.exp(jnp.arange(width // 2, dtype=jnp.float32) * (-2.0 * math.log(rope_base) / width))
    angles = offset.astype(jnp.float32)[:, None] * frequency[None, :]
    return (jnp.cos(angles), jnp.sin(angles))

def doc_layout(doc_lengths, places):
    doc_ends = jnp.cumsum(doc_lengths).astype(jnp.int32)
    starts = (doc_ends - doc_lengths).astype(jnp.int32)
    doc_ids = lax.optimization_barrier(jnp.sum((places[:, None] >= doc_ends[None, :]).astype(jnp.int32), axis=1)).astype(jnp.int32)
    numbers = jnp.arange(doc_lengths.shape[0], dtype=jnp.int32)
    first_place = lax.optimization_barrier(jnp.sum(jnp.where(doc_ids[:, None] == numbers[None, :], starts[None, :], 0), axis=1)).astype(jnp.int32)
    return (doc_ids, (places - first_place).astype(jnp.int32))

def window_mask(query_docs, query_places, key_docs, key_places):
    gap_rows = query_places[:, None] - key_places[None, :]
    same_doc = query_docs[:, None] == key_docs[None, :]
    return same_doc & (key_places[None, :] >= 0) & (gap_rows >= 0) & (gap_rows < WINDOW)

def layer(inputs, params, doc_ids, offset, places):
    query_weight, key_weight, value_weight, out_weight, gate_weight, up_weight, down_weight, norm_gain, head_gain = params
    row_count = inputs.shape[0]
    cosine, sine_table = angle_tables(offset, HD)
    normed_in = low(rms_scale(inputs, norm_gain[0]))
    query_proj = low_back(exact_dot(normed_in, query_weight)).reshape(row_count, H, HD)
    key_proj = low_back(exact_dot(normed_in, key_weight))
    value_proj = low(low_back(exact_dot(normed_in, value_weight)))
    query_rot = low(rotate(rms_scale(query_proj, head_gain[0]), cosine[:, None, :], sine_table[:, None, :]))
    key_rot = low(rotate(rms_scale(key_proj, head_gain[1]), cosine, sine_table))
    raw_scores = low_back(jnp.einsum('qhd,kd->hqk', query_rot, key_rot, precision=lax.Precision.HIGHEST) * HD ** (-0.5))
    allowed = window_mask(doc_ids, places, doc_ids, places)
    scores = jnp.where(allowed[None], raw_scores, neg_fill)
    row_max = lax.optimization_barrier(jnp.max(scores, axis=-1, keepdims=True))
    log_total = row_max + jnp.log(lax.optimization_barrier(jnp.sum(jnp.exp(scores - row_max), axis=-1, keepdims=True)))
    soft_probs = low(jnp.exp(scores - log_total))
    mixed = jnp.einsum('hqk,kd->qhd', soft_probs, value_proj, precision=lax.Precision.HIGHEST)
    mixed = low(low_back(mixed.reshape(row_count, H * HD)))
    attn_proj = low_back(exact_dot(mixed, out_weight))
    residual = inputs + rms_scale(attn_proj, norm_gain[1])
    ff_in = low(rms_scale(residual, norm_gain[2]))
    gate_proj = low_back(exact_dot(ff_in, gate_weight))
    up_proj = low_back(exact_dot(ff_in, up_weight))
    hidden = low(low_back(gelu_tanh(gate_proj) * up_proj))
    ff_out = low_back(exact_dot(hidden, down_weight))
    return residual + rms_scale(ff_out, norm_gain[3])

def reference(tokens, cotangent, lengths, query_weight, key_weight, value_weight, out_weight, gate_weight, up_weight, down_weight, norm_gains, head_gains):
    params = tuple((weight.astype(jnp.float32) for weight in (query_weight, key_weight, value_weight, out_weight, gate_weight, up_weight, down_weight, norm_gains, head_gains)))
    places = jnp.arange(TOK_GROUP, dtype=jnp.int32)
    flat_tokens = tokens.reshape(MICRO * GROUPS, TOK_GROUP, D)
    flat_grads = cotangent.reshape(MICRO * GROUPS, TOK_GROUP, D)
    flat_lengths = lengths.reshape(MICRO * GROUPS, NDOC)

    def one_item(running, inputs):
        sequence, out_grad, doc_lengths = inputs
        doc_ids, offset = doc_layout(doc_lengths, places)

        def both_layers(section_in, probe, weights):
            lower = tuple((weight[0] for weight in weights))
            upper = tuple((weight[1] for weight in weights))
            first_out = low(low_back(layer(section_in, lower, doc_ids, offset, places)))
            second_out = layer(first_out + probe, upper, doc_ids, offset, places)
            return (first_out, second_out)
        section_in = sequence.astype(jnp.float32)
        probe = jnp.zeros_like(section_in)
        outputs, back = jax.vjp(both_layers, section_in, probe, params)
        grad_in, grad_probe, grad_params = back((jnp.zeros_like(outputs[0]), out_grad.astype(jnp.float32)))
        running = jax.tree.map(lambda held, fresh: held + fresh, running, grad_params)
        return (running, (outputs[0].astype(jnp.bfloat16), outputs[1].astype(jnp.bfloat16), grad_in, grad_probe))
    zeros = tuple((jnp.zeros_like(weight) for weight in params))
    running, stacked = lax.scan(one_item, zeros, (flat_tokens, flat_grads, flat_lengths))
    section_out = jnp.stack([stacked[0], stacked[1]]).reshape(2, MICRO, GROUPS, TOK_GROUP, D)
    input_grad = jnp.stack([stacked[2], stacked[3]]).reshape(2, MICRO, GROUPS, TOK_GROUP, D)
    return (section_out, input_grad, running[0], running[1], running[2], running[3], running[4], running[5], running[6], running[7], running[8])
```

```python
import math

import jax
import jax.numpy as jnp
from jax import lax
from jax.sharding import PartitionSpec as P

WINDOW = 512


epsilon = 1e-06
rope_base = 10000.0
neg_fill = -1e30
gelu_coef = 0.7978845608028654


def from_behind(block, axis, distance):
    devices = range(lax.axis_size(axis))
    route = [(i - distance, i) for i in devices if i - distance in devices]
    return lax.ppermute(block, axis, route)


def rms_scale(vector, gain_vec):
    return (
        vector * lax.rsqrt(jnp.mean(vector * vector, axis=-1, keepdims=True) + epsilon) * gain_vec
    )


def gelu_tanh(vector):
    return (
        0.5 * vector * (1.0 + jnp.tanh(gelu_coef * (vector + 0.044715 * vector * vector * vector)))
    )


def geglu(gate_proj, up_proj):
    return gelu_tanh(gate_proj) * up_proj


def rotate(vector, cosine, sine_table):
    half_width = vector.shape[-1] // 2
    first_half = vector[..., :half_width]
    second_half = vector[..., half_width:]
    return jnp.concatenate(
        [
            first_half * cosine - second_half * sine_table,
            second_half * cosine + first_half * sine_table,
        ],
        axis=-1,
    )


def angle_tables(offset, width):
    frequency = jnp.exp(
        jnp.arange(width // 2, dtype=jnp.float32) * (-2.0 * math.log(rope_base) / width)
    )
    angles = offset.astype(jnp.float32)[:, None] * frequency[None, :]
    return (jnp.cos(angles), jnp.sin(angles))


def doc_layout(doc_lengths, places):
    doc_ends = jnp.cumsum(doc_lengths)
    starts = doc_ends - doc_lengths
    doc_ids = jnp.sum((places[:, None] >= doc_ends[None, :]).astype(jnp.int32), axis=1)
    numbers = jnp.arange(doc_lengths.shape[0], dtype=jnp.int32)
    first_place = jnp.sum(
        jnp.where(doc_ids[:, None] == numbers[None, :], starts[None, :], 0), axis=1
    )
    return (doc_ids, places - first_place)


def window_mask(query_docs, query_places, key_docs, key_places):
    gap_rows = query_places[:, None] - key_places[None, :]
    same_doc = query_docs[:, None] == key_docs[None, :]
    return same_doc & (key_places[None, :] >= 0) & (gap_rows >= 0) & (gap_rows < WINDOW)


def outer_dot(left, right):
    return lax.dot_general(
        left, right, (((0,), (0,)), ((), ())), preferred_element_type=jnp.float32
    )


def dot_transposed(left, right):
    return lax.dot_general(
        left, right, (((1,), (1,)), ((), ())), preferred_element_type=jnp.float32
    )


def pullback(function, first_arg, second_arg, grad_value):
    unused, back = jax.vjp(function, first_arg, second_arg)
    return back(grad_value)


def block_scores(query_heads, key_block, allowed, scale_factor):
    raw_scores = (
        jnp.einsum("hqd,kd->hqk", query_heads, key_block, preferred_element_type=jnp.float32)
        * scale_factor
    )
    return jnp.where(allowed[None], raw_scores, neg_fill)


def bit_pair():
    second_core = lax.axis_index("section") == 1
    first_bit = jnp.where(second_core, 2, 1)
    return (first_bit, 3 - first_bit)


def hop(block, stage):
    size = lax.axis_size("fsdp")
    route = []
    for core in range(2):
        bit = 1 if core == stage else 2
        for place in range(size):
            route.append((core * size + place, core * size + (place ^ bit)))
    return lax.ppermute(block, ("section", "fsdp"), route)


def swap_cores(block):
    return lax.ppermute(block, "section", [(0, 1), (1, 0)])


def ordered(mine, other, axis):
    first_core = lax.axis_index("section") == 0
    return jnp.concatenate(
        [jnp.where(first_core, mine, other), jnp.where(first_core, other, mine)], axis=axis
    )


def gather_rows(block):
    me = lax.axis_index("fsdp")
    first_bit, second_bit = bit_pair()
    near = hop(block, 0)
    side = hop(block, 1)
    far = hop(near, 1)
    held = jnp.zeros((lax.axis_size("fsdp"),) + block.shape, block.dtype)
    for piece, place in (
        (block, me),
        (near, me ^ first_bit),
        (side, me ^ second_bit),
        (far, me ^ 3),
    ):
        held = lax.dynamic_update_index_in_dim(held, piece, place, 0)
    return (held, swap_cores(held))


def join_rows(pair, columns):
    mine, other = pair
    mine = mine[:, None, :, columns]
    other = other[:, None, :, columns]
    whole = ordered(mine, other, 1)
    return whole.reshape(-1, whole.shape[-1])


def scatter_rows(grad):
    core = lax.axis_index("section")
    me = lax.axis_index("fsdp")
    first_bit, second_bit = bit_pair()
    size = lax.axis_size("fsdp")
    blocks = grad.reshape(size, 2, grad.shape[0] // (2 * size), grad.shape[1])

    def pick(source, place):
        return lax.dynamic_index_in_dim(source, place, 0, keepdims=False)

    arrived = swap_cores(lax.dynamic_index_in_dim(blocks, 1 - core, 1, keepdims=False))
    kept = lax.dynamic_index_in_dim(blocks, core, 1, keepdims=False)
    total = kept.astype(jnp.float32) + arrived.astype(jnp.float32)
    near = hop(
        jnp.stack([pick(total, me ^ first_bit), pick(total, me ^ 3)]).astype(jnp.bfloat16), 0
    ).astype(jnp.float32)
    far = hop((pick(total, me ^ second_bit) + near[1]).astype(jnp.bfloat16), 1)
    return pick(total, me) + near[0] + far.astype(jnp.float32)


def layer_forward(inputs, params, layout):
    qkv_weight, out_weight, gu_weight, down_weight, norm_gain, head_gain = params
    allowed_own, allowed_prior, cosine, sine_table = layout
    row_count = inputs.shape[0]
    head_size = head_gain.shape[1]
    query_width = out_weight.shape[0]
    head_count = query_width // head_size
    ff_width = down_weight.shape[0]
    scale_factor = head_size ** (-0.5)
    normed_in = rms_scale(inputs, norm_gain[0]).astype(jnp.bfloat16)
    kv_proj = jnp.dot(
        normed_in, qkv_weight[:, query_width:], preferred_element_type=jnp.float32
    )
    key_proj = kv_proj[:, :head_size]
    value_proj = kv_proj[:, head_size:].astype(jnp.bfloat16)
    key_rot = rotate(rms_scale(key_proj, head_gain[1]), cosine, sine_table).astype(jnp.bfloat16)
    prior_rows = from_behind(jnp.concatenate([key_rot, value_proj], axis=1), "fsdp", 1)
    query_proj = jnp.dot(
        normed_in, qkv_weight[:, :query_width], preferred_element_type=jnp.float32
    ).reshape(row_count, head_count, head_size)
    query_rot = rotate(
        rms_scale(query_proj, head_gain[0]), cosine[:, None, :], sine_table[:, None, :]
    ).astype(jnp.bfloat16)
    prior_keys = prior_rows[:, :head_size]
    prior_values = prior_rows[:, head_size:]
    query_heads = query_rot.transpose(1, 0, 2)
    scores_own = block_scores(query_heads, key_rot, allowed_own, scale_factor)
    scores_prior = block_scores(query_heads, prior_keys, allowed_prior, scale_factor)
    row_max = jnp.maximum(
        jnp.max(scores_own, axis=-1, keepdims=True), jnp.max(scores_prior, axis=-1, keepdims=True)
    )
    exp_own = jnp.exp(scores_own - row_max)
    exp_prior = jnp.exp(scores_prior - row_max)
    inverse = 1.0 / (
        jnp.sum(exp_own, axis=-1, keepdims=True) + jnp.sum(exp_prior, axis=-1, keepdims=True)
    )
    probs_own = (exp_own * inverse).astype(jnp.bfloat16)
    probs_prior = (exp_prior * inverse).astype(jnp.bfloat16)
    mixed_heads = jnp.einsum(
        "hqk,kd->hqd", probs_own, value_proj, preferred_element_type=jnp.float32
    ) + jnp.einsum("hqk,kd->hqd", probs_prior, prior_values, preferred_element_type=jnp.float32)
    mixed = mixed_heads.transpose(1, 0, 2).reshape(row_count, query_width).astype(jnp.bfloat16)
    attn_proj = jnp.dot(mixed, out_weight, preferred_element_type=jnp.float32)
    residual = inputs + rms_scale(attn_proj, norm_gain[1])
    ff_in = rms_scale(residual, norm_gain[2]).astype(jnp.bfloat16)
    gate_proj = jnp.dot(ff_in, gu_weight[:, :ff_width], preferred_element_type=jnp.float32)
    up_proj = jnp.dot(ff_in, gu_weight[:, ff_width:], preferred_element_type=jnp.float32)
    hidden = geglu(gate_proj, up_proj).astype(jnp.bfloat16)
    ff_out = jnp.dot(hidden, down_weight, preferred_element_type=jnp.float32)
    outputs = residual + rms_scale(ff_out, norm_gain[3])
    kept_state = (
        inputs,
        normed_in,
        query_proj,
        key_proj,
        query_heads,
        key_rot,
        value_proj,
        prior_keys,
        prior_values,
        probs_own,
        probs_prior,
        mixed,
        attn_proj,
        residual,
        ff_in,
        gate_proj,
        up_proj,
        hidden,
        ff_out,
    )
    return (outputs, kept_state)


def layer_backward(grad_out, kept_state, params, layout):
    qkv_weight, out_weight, gu_weight, down_weight, norm_gain, head_gain = params
    unused_own, unused_prior, cosine, sine_table = layout
    (
        inputs,
        normed_in,
        query_proj,
        key_proj,
        query_heads,
        key_rot,
        value_proj,
        prior_keys,
        prior_values,
        probs_own,
        probs_prior,
        mixed,
        attn_proj,
        residual,
        ff_in,
        gate_proj,
        up_proj,
        hidden,
        ff_out,
    ) = kept_state
    row_count = inputs.shape[0]
    head_size = head_gain.shape[1]
    query_width = out_weight.shape[0]
    head_count = query_width // head_size
    scale_factor = head_size ** (-0.5)
    d_ff_out, grad_post_ff = pullback(rms_scale, ff_out, norm_gain[3], grad_out)
    d_ff_out = d_ff_out.astype(jnp.bfloat16)
    grad_down = outer_dot(hidden, d_ff_out).astype(jnp.bfloat16)
    d_hidden = dot_transposed(d_ff_out, down_weight).astype(jnp.bfloat16)
    d_gate, d_up = pullback(geglu, gate_proj, up_proj, d_hidden.astype(jnp.float32))
    d_gate_up = jnp.concatenate([d_gate.astype(jnp.bfloat16), d_up.astype(jnp.bfloat16)], axis=1)
    grad_gate_up = outer_dot(ff_in, d_gate_up).astype(jnp.bfloat16)
    d_ff_in = dot_transposed(d_gate_up, gu_weight)
    d_resid_part, grad_pre_ff = pullback(rms_scale, residual, norm_gain[2], d_ff_in)
    d_residual = grad_out + d_resid_part
    d_attn, grad_post_attn = pullback(rms_scale, attn_proj, norm_gain[1], d_residual)
    d_attn = d_attn.astype(jnp.bfloat16)
    grad_out_proj = outer_dot(mixed, d_attn).astype(jnp.bfloat16)
    d_mixed = dot_transposed(d_attn, out_weight).astype(jnp.bfloat16)
    d_mixed_heads = d_mixed.reshape(row_count, head_count, head_size).transpose(1, 0, 2)
    row_dots = jnp.sum(
        (d_mixed.astype(jnp.float32) * mixed.astype(jnp.float32)).reshape(
            row_count, head_count, head_size
        ),
        axis=-1,
    ).T[:, :, None]

    def against(keys, values, probs):
        d_values = jnp.einsum(
            "hqk,hqd->kd", probs, d_mixed_heads, preferred_element_type=jnp.float32
        )
        d_probs = jnp.einsum(
            "hqd,kd->hqk", d_mixed_heads, values, preferred_element_type=jnp.float32
        )
        d_scores = (probs.astype(jnp.float32) * (d_probs - row_dots)).astype(jnp.bfloat16)
        d_keys = (
            jnp.einsum("hqk,hqd->kd", d_scores, query_heads, preferred_element_type=jnp.float32)
            * scale_factor
        )
        return (d_keys, d_values, d_scores)

    d_prior_keys, d_prior_values, d_prior_scores = against(prior_keys, prior_values, probs_prior)
    returned = from_behind(
        jnp.concatenate([d_prior_keys, d_prior_values], axis=1).astype(jnp.bfloat16), "fsdp", -1
    ).astype(jnp.float32)
    d_own_keys, d_own_values, d_own_scores = against(key_rot, value_proj, probs_own)
    d_query_heads = (
        jnp.einsum("hqk,kd->hqd", d_own_scores, key_rot, preferred_element_type=jnp.float32)
        + jnp.einsum("hqk,kd->hqd", d_prior_scores, prior_keys, preferred_element_type=jnp.float32)
    ) * scale_factor
    d_query_rows = d_query_heads.transpose(1, 0, 2)
    d_key_rot = d_own_keys + returned[:, :head_size]
    d_value = (d_own_values + returned[:, head_size:]).astype(jnp.bfloat16)

    def query_head(vector, gain_vec):
        return rotate(rms_scale(vector, gain_vec), cosine[:, None, :], sine_table[:, None, :])

    def key_head(vector, gain_vec):
        return rotate(rms_scale(vector, gain_vec), cosine, sine_table)

    d_query, grad_query_gain = pullback(query_head, query_proj, head_gain[0], d_query_rows)
    d_key, grad_key_gain = pullback(key_head, key_proj, head_gain[1], d_key_rot)
    d_query = d_query.reshape(row_count, query_width).astype(jnp.bfloat16)
    d_qkv = jnp.concatenate([d_query, d_key.astype(jnp.bfloat16), d_value], axis=1)
    grad_qkv = outer_dot(normed_in, d_qkv).astype(jnp.bfloat16)
    d_normed = dot_transposed(d_qkv, qkv_weight)
    d_input_part, grad_in_gain = pullback(rms_scale, inputs, norm_gain[0], d_normed)
    d_inputs = d_residual + d_input_part
    gain_grads = jnp.concatenate(
        [grad_in_gain, grad_post_attn, grad_pre_ff, grad_post_ff, grad_query_gain, grad_key_gain]
    )
    return (d_inputs, (grad_qkv, grad_out_proj, grad_gate_up, grad_down), gain_grads)


def local(
    tokens,
    cotangent,
    lengths,
    query_weight,
    key_weight,
    value_weight,
    out_weight,
    gate_weight,
    up_weight,
    down_weight,
    norm_gains,
    head_gains,
):
    core = lax.axis_index("section")
    me = lax.axis_index("fsdp")
    first_core = core == 0
    row_count = tokens.shape[2]
    width = tokens.shape[3]
    query_width = query_weight.shape[2]
    head_size = key_weight.shape[2]
    qkv_width = query_width + 2 * head_size
    ff_width = gate_weight.shape[2]
    out_rows = out_weight.shape[1] // 2

    gain_count, gain_share = norm_gains.shape[1:]
    head_share = head_gains.shape[2]
    packed_gains = jnp.concatenate(
        [norm_gains.reshape(1, -1), head_gains.reshape(1, -1)], axis=1
    )[:, None]
    packed_gains = lax.all_gather(packed_gains, ("section", "fsdp"), axis=0).reshape(
        2, lax.axis_size("fsdp"), -1
    )
    split_at = gain_count * gain_share
    all_norms = (
        packed_gains[:, :, :split_at]
        .reshape(2, -1, gain_count, gain_share)
        .transpose(0, 2, 1, 3)
        .reshape(2, gain_count, -1)
        .astype(jnp.float32)
    )
    all_heads = (
        packed_gains[:, :, split_at:]
        .reshape(2, -1, 2, head_share)
        .transpose(0, 2, 1, 3)
        .reshape(2, 2, -1)
        .astype(jnp.float32)
    )

    wide = jnp.concatenate(
        [query_weight[0], key_weight[0], value_weight[0], gate_weight[0], up_weight[0]], axis=1
    )
    wide = wide.reshape(2, -1, wide.shape[1])
    narrow = jnp.concatenate(
        [
            out_weight[0].reshape(2, -1, width),
            down_weight[0].reshape(2, -1, width),
        ],
        axis=1,
    )
    layer_blocks = []
    for packed in (wide, narrow):
        arrived = swap_cores(lax.dynamic_index_in_dim(packed, 1 - core, 0, keepdims=False))
        kept = lax.dynamic_index_in_dim(packed, core, 0, keepdims=False)
        layer_blocks.append(
            (jnp.where(first_core, kept, arrived), jnp.where(first_core, arrived, kept))
        )
    params = []
    for index_l in range(2):
        wide_pair = gather_rows(layer_blocks[0][index_l])
        narrow_pair = gather_rows(layer_blocks[1][index_l])
        everything = slice(None)
        narrow_out = tuple(piece[:, :out_rows] for piece in narrow_pair)
        narrow_down = tuple(piece[:, out_rows:] for piece in narrow_pair)
        params.append(
            (
                join_rows(wide_pair, slice(0, qkv_width)),
                join_rows(narrow_out, everything),
                join_rows(wide_pair, slice(qkv_width, None)),
                join_rows(narrow_down, everything),
                all_norms[index_l],
                all_heads[index_l],
            )
        )

    def own_micro(rows):
        return lax.dynamic_index_in_dim(rows, core, 0, keepdims=False)[0]

    doc_lengths = own_micro(lengths)
    places = me * row_count + jnp.arange(row_count, dtype=jnp.int32)
    prior_places = places - row_count
    doc_ids, offset = doc_layout(doc_lengths, places)
    prior_docs, unused = doc_layout(doc_lengths, prior_places)
    layout = (
        window_mask(doc_ids, places, doc_ids, places),
        window_mask(doc_ids, places, prior_docs, prior_places),
    ) + angle_tables(offset, head_size)

    lower_out, lower_state = layer_forward(
        own_micro(tokens).astype(jnp.float32), params[0], layout
    )
    lower_out = lower_out.astype(jnp.bfloat16)
    upper_out, upper_state = layer_forward(lower_out.astype(jnp.float32), params[1], layout)
    upper_out = upper_out.astype(jnp.bfloat16)

    d_middle, upper_grads, upper_gains = layer_backward(
        own_micro(cotangent).astype(jnp.float32), upper_state, params[1], layout
    )
    upper_sums = [scatter_rows(grad).astype(jnp.bfloat16) for grad in upper_grads]
    upper_sums = [lax.psum(total, "rep") for total in upper_sums]
    d_tokens, lower_grads, lower_gains = layer_backward(
        d_middle.astype(jnp.bfloat16).astype(jnp.float32), lower_state, params[0], layout
    )
    lower_sums = [scatter_rows(grad).astype(jnp.bfloat16) for grad in lower_grads]
    lower_sums, upper_sums = lax.optimization_barrier((lower_sums, upper_sums))
    lower_sums = [lax.psum(total, "rep") for total in lower_sums]

    def for_layers(lower_value, upper_value):
        mine = jnp.where(first_core, lower_value, upper_value)
        theirs = jnp.where(first_core, upper_value, lower_value)
        return (mine, swap_cores(theirs.astype(jnp.bfloat16)).astype(mine.dtype))

    section_out = ordered(*(rows[None] for rows in for_layers(lower_out, upper_out)), 0)
    input_grad = ordered(*(rows[None] for rows in for_layers(d_tokens, d_middle)), 0)
    shares = [
        ordered(*for_layers(lower_sum, upper_sum), 0).astype(jnp.float32)[None]
        for lower_sum, upper_sum in zip(lower_sums, upper_sums)
    ]
    gain_sums = lax.psum(jnp.stack([lower_gains, upper_gains]), ("section", "fsdp", "rep"))
    gain_sums = lax.dynamic_index_in_dim(gain_sums, core, 0, keepdims=True)
    norm_sums = gain_sums[:, : gain_count * width].reshape(1, gain_count, width)
    head_sums = gain_sums[:, gain_count * width :].reshape(1, 2, head_size)
    norm_sums = lax.dynamic_slice_in_dim(norm_sums, me * gain_share, gain_share, 2)
    head_sums = lax.dynamic_slice_in_dim(head_sums, me * head_share, head_share, 2)
    qkv_share, out_share, gate_up_share, down_share = shares
    return (
        section_out[None, :, None],
        input_grad[None, :, None],
        qkv_share[:, :, :query_width],
        qkv_share[:, :, query_width : query_width + head_size],
        qkv_share[:, :, query_width + head_size :],
        out_share,
        gate_up_share[:, :, :ff_width],
        gate_up_share[:, :, ff_width:],
        down_share,
        norm_sums,
        head_sums,
    )


def solution(mesh):
    return jax.shard_map(
        local,
        mesh=mesh,
        in_specs=(
            P(None, "rep", "fsdp", None),
            P(None, "rep", "fsdp", None),
            P(None, "rep", None),
            P("section", "fsdp", None),
            P("section", "fsdp", None),
            P("section", "fsdp", None),
            P("section", "fsdp", None),
            P("section", "fsdp", None),
            P("section", "fsdp", None),
            P("section", "fsdp", None),
            P("section", None, "fsdp"),
            P("section", None, "fsdp"),
        ),
        out_specs=(
            P("section", None, "rep", "fsdp", None),
            P("section", None, "rep", "fsdp", None),
            P("section", "fsdp", None),
            P("section", "fsdp", None),
            P("section", "fsdp", None),
            P("section", "fsdp", None),
            P("section", "fsdp", None),
            P("section", "fsdp", None),
            P("section", "fsdp", None),
            P("section", None, "fsdp"),
            P("section", None, "fsdp"),
        ),
        check_vma=False,
    )
```

```python
import math

import jax
import jax.numpy as jnp
from jax import lax
from jax.sharding import PartitionSpec as P

WINDOW = 512


epsilon = 1e-06
rope_base = 10000.0
neg_fill = -1e30
gelu_coef = 0.7978845608028654


def from_behind(block, axis, distance):
    devices = range(lax.axis_size(axis))
    route = [(i - distance, i) for i in devices if i - distance in devices]
    return lax.ppermute(block, axis, route)


def rms_scale(vector, gain_vec):
    return (
        vector * lax.rsqrt(jnp.mean(vector * vector, axis=-1, keepdims=True) + epsilon) * gain_vec
    )


def gelu_tanh(vector):
    return (
        0.5 * vector * (1.0 + jnp.tanh(gelu_coef * (vector + 0.044715 * vector * vector * vector)))
    )


def geglu(gate_proj, up_proj):
    return gelu_tanh(gate_proj) * up_proj


def rotate(vector, cosine, sine_table):
    half_width = vector.shape[-1] // 2
    first_half = vector[..., :half_width]
    second_half = vector[..., half_width:]
    return jnp.concatenate(
        [
            first_half * cosine - second_half * sine_table,
            second_half * cosine + first_half * sine_table,
        ],
        axis=-1,
    )


def angle_tables(offset, width):
    frequency = jnp.exp(
        jnp.arange(width // 2, dtype=jnp.float32) * (-2.0 * math.log(rope_base) / width)
    )
    angles = offset.astype(jnp.float32)[:, None] * frequency[None, :]
    return (jnp.cos(angles), jnp.sin(angles))


def doc_layout(doc_lengths, places):
    doc_ends = jnp.cumsum(doc_lengths)
    starts = doc_ends - doc_lengths
    doc_ids = jnp.sum((places[:, None] >= doc_ends[None, :]).astype(jnp.int32), axis=1)
    numbers = jnp.arange(doc_lengths.shape[0], dtype=jnp.int32)
    first_place = jnp.sum(
        jnp.where(doc_ids[:, None] == numbers[None, :], starts[None, :], 0), axis=1
    )
    return (doc_ids, places - first_place)


def window_mask(query_docs, query_places, key_docs, key_places):
    gap_rows = query_places[:, None] - key_places[None, :]
    same_doc = query_docs[:, None] == key_docs[None, :]
    return same_doc & (key_places[None, :] >= 0) & (gap_rows >= 0) & (gap_rows < WINDOW)


def outer_dot(left, right):
    return lax.dot_general(
        left, right, (((0,), (0,)), ((), ())), preferred_element_type=jnp.float32
    )


def dot_transposed(left, right):
    return lax.dot_general(
        left, right, (((1,), (1,)), ((), ())), preferred_element_type=jnp.float32
    )


def pullback(function, first_arg, second_arg, grad_value):
    unused, back = jax.vjp(function, first_arg, second_arg)
    return back(grad_value)


def block_scores(query_heads, key_block, allowed, scale_factor):
    raw_scores = (
        jnp.einsum("hqd,kd->hqk", query_heads, key_block, preferred_element_type=jnp.float32)
        * scale_factor
    )
    return jnp.where(allowed[None], raw_scores, neg_fill)


def bit_pair():
    second_core = lax.axis_index("section") == 1
    first_bit = jnp.where(second_core, 2, 1)
    return (first_bit, 3 - first_bit)


def hop(block, stage):
    size = lax.axis_size("fsdp")
    route = []
    for core in range(2):
        bit = 1 if core == stage else 2
        for place in range(size):
            route.append((core * size + place, core * size + (place ^ bit)))
    return lax.ppermute(block, ("section", "fsdp"), route)


def swap_cores(block):
    return lax.ppermute(block, "section", [(0, 1), (1, 0)])


def ordered(mine, other, axis):
    first_core = lax.axis_index("section") == 0
    return jnp.concatenate(
        [jnp.where(first_core, mine, other), jnp.where(first_core, other, mine)], axis=axis
    )


def near_rows(block):
    return (block, hop(block, 0), hop(block, 1))


def gather_rows(pieces):
    block, near, side = pieces
    me = lax.axis_index("fsdp")
    first_bit, second_bit = bit_pair()
    far = hop(near, 1)
    held = jnp.zeros((lax.axis_size("fsdp"),) + block.shape, block.dtype)
    for piece, place in (
        (block, me),
        (near, me ^ first_bit),
        (side, me ^ second_bit),
        (far, me ^ 3),
    ):
        held = lax.dynamic_update_index_in_dim(held, piece, place, 0)
    return held


def join_rows(pair, columns):
    mine, other = pair
    mine = mine[:, None, :, columns]
    other = other[:, None, :, columns]
    whole = ordered(mine, other, 1)
    return whole.reshape(-1, whole.shape[-1])


def pick(source, place):
    return lax.dynamic_index_in_dim(source, place, 0, keepdims=False)


def row_blocks(grad):
    size = lax.axis_size("fsdp")
    return grad.reshape(size, 2, grad.shape[0] // (2 * size), grad.shape[1])


def add_cores(blocks):
    core = lax.axis_index("section")
    arrived = swap_cores(lax.dynamic_index_in_dim(blocks, 1 - core, 1, keepdims=False))
    kept = lax.dynamic_index_in_dim(blocks, core, 1, keepdims=False)
    return kept.astype(jnp.float32) + arrived.astype(jnp.float32)


def add_near(total):
    me = lax.axis_index("fsdp")
    first_bit, second_bit = bit_pair()
    near = hop(
        jnp.stack([pick(total, me ^ first_bit), pick(total, me ^ 3)]).astype(jnp.bfloat16), 0
    ).astype(jnp.float32)
    return (
        pick(total, me) + near[0],
        (pick(total, me ^ second_bit) + near[1]).astype(jnp.bfloat16),
    )


def add_far(pair):
    return (pair[0] + hop(pair[1], 1).astype(jnp.float32)).astype(jnp.bfloat16)


def layer_forward(inputs, params, layout, pending):
    qkv_weight, out_weight, gu_weight, down_weight, norm_gain, head_gain = params
    allowed_own, allowed_prior, cosine, sine_table = layout
    row_count = inputs.shape[0]
    head_size = head_gain.shape[1]
    query_width = out_weight.shape[0]
    head_count = query_width // head_size
    ff_width = down_weight.shape[0]
    scale_factor = head_size ** (-0.5)
    normed_in = rms_scale(inputs, norm_gain[0]).astype(jnp.bfloat16)
    kv_proj = jnp.dot(
        normed_in, qkv_weight[:, query_width:], preferred_element_type=jnp.float32
    )
    key_proj = kv_proj[:, :head_size]
    value_proj = kv_proj[:, head_size:].astype(jnp.bfloat16)
    key_rot = rotate(rms_scale(key_proj, head_gain[1]), cosine, sine_table).astype(jnp.bfloat16)
    prior_rows = from_behind(jnp.concatenate([key_rot, value_proj], axis=1), "fsdp", 1)
    query_proj = jnp.dot(
        normed_in, qkv_weight[:, :query_width], preferred_element_type=jnp.float32
    ).reshape(row_count, head_count, head_size)
    query_rot = rotate(
        rms_scale(query_proj, head_gain[0]), cosine[:, None, :], sine_table[:, None, :]
    ).astype(jnp.bfloat16)
    prior_keys = prior_rows[:, :head_size]
    prior_values = prior_rows[:, head_size:]
    query_heads = query_rot.transpose(1, 0, 2)
    scores_own = block_scores(query_heads, key_rot, allowed_own, scale_factor)
    scores_prior = block_scores(query_heads, prior_keys, allowed_prior, scale_factor)
    row_max = jnp.maximum(
        jnp.max(scores_own, axis=-1, keepdims=True), jnp.max(scores_prior, axis=-1, keepdims=True)
    )
    exp_own = jnp.exp(scores_own - row_max)
    exp_prior = jnp.exp(scores_prior - row_max)
    inverse = 1.0 / (
        jnp.sum(exp_own, axis=-1, keepdims=True) + jnp.sum(exp_prior, axis=-1, keepdims=True)
    )
    probs_own = (exp_own * inverse).astype(jnp.bfloat16)
    probs_prior = (exp_prior * inverse).astype(jnp.bfloat16)
    mixed_heads = jnp.einsum(
        "hqk,kd->hqd", probs_own, value_proj, preferred_element_type=jnp.float32
    ) + jnp.einsum("hqk,kd->hqd", probs_prior, prior_values, preferred_element_type=jnp.float32)
    mixed = mixed_heads.transpose(1, 0, 2).reshape(row_count, query_width).astype(jnp.bfloat16)
    attn_proj = jnp.dot(mixed, out_weight, preferred_element_type=jnp.float32)
    residual = inputs + rms_scale(attn_proj, norm_gain[1])
    residual, pending = lax.optimization_barrier((residual, pending))
    ff_in = rms_scale(residual, norm_gain[2]).astype(jnp.bfloat16)
    gate_proj = jnp.dot(ff_in, gu_weight[:, :ff_width], preferred_element_type=jnp.float32)
    up_proj = jnp.dot(ff_in, gu_weight[:, ff_width:], preferred_element_type=jnp.float32)
    hidden = geglu(gate_proj, up_proj).astype(jnp.bfloat16)
    ff_out = jnp.dot(hidden, down_weight, preferred_element_type=jnp.float32)
    outputs = residual + rms_scale(ff_out, norm_gain[3])
    kept_state = (
        inputs,
        normed_in,
        query_proj,
        key_proj,
        query_heads,
        key_rot,
        value_proj,
        prior_keys,
        prior_values,
        probs_own,
        probs_prior,
        mixed,
        attn_proj,
        residual,
        ff_in,
        gate_proj,
        up_proj,
        hidden,
        ff_out,
    )
    return (outputs, kept_state, pending)


def ff_backward(grad_out, kept_state, params):
    qkv_weight, out_weight, gu_weight, down_weight, norm_gain, head_gain = params
    (
        inputs,
        normed_in,
        query_proj,
        key_proj,
        query_heads,
        key_rot,
        value_proj,
        prior_keys,
        prior_values,
        probs_own,
        probs_prior,
        mixed,
        attn_proj,
        residual,
        ff_in,
        gate_proj,
        up_proj,
        hidden,
        ff_out,
    ) = kept_state
    d_ff_out, grad_post_ff = pullback(rms_scale, ff_out, norm_gain[3], grad_out)
    d_ff_out = d_ff_out.astype(jnp.bfloat16)
    grad_down = outer_dot(hidden, d_ff_out).astype(jnp.bfloat16)
    d_hidden = dot_transposed(d_ff_out, down_weight).astype(jnp.bfloat16)
    d_gate, d_up = pullback(geglu, gate_proj, up_proj, d_hidden.astype(jnp.float32))
    d_gate_up = jnp.concatenate([d_gate.astype(jnp.bfloat16), d_up.astype(jnp.bfloat16)], axis=1)
    grad_gate_up = outer_dot(ff_in, d_gate_up).astype(jnp.bfloat16)
    d_ff_in = dot_transposed(d_gate_up, gu_weight)
    d_resid_part, grad_pre_ff = pullback(rms_scale, residual, norm_gain[2], d_ff_in)
    d_residual = grad_out + d_resid_part
    return (d_residual, (grad_gate_up, grad_down), (grad_pre_ff, grad_post_ff))


def attn_backward(d_residual, kept_state, params, layout):
    qkv_weight, out_weight, gu_weight, down_weight, norm_gain, head_gain = params
    unused_own, unused_prior, cosine, sine_table = layout
    (
        inputs,
        normed_in,
        query_proj,
        key_proj,
        query_heads,
        key_rot,
        value_proj,
        prior_keys,
        prior_values,
        probs_own,
        probs_prior,
        mixed,
        attn_proj,
        residual,
        ff_in,
        gate_proj,
        up_proj,
        hidden,
        ff_out,
    ) = kept_state
    row_count = inputs.shape[0]
    head_size = head_gain.shape[1]
    query_width = out_weight.shape[0]
    head_count = query_width // head_size
    scale_factor = head_size ** (-0.5)
    d_attn, grad_post_attn = pullback(rms_scale, attn_proj, norm_gain[1], d_residual)
    d_attn = d_attn.astype(jnp.bfloat16)
    grad_out_proj = outer_dot(mixed, d_attn).astype(jnp.bfloat16)
    d_mixed = dot_transposed(d_attn, out_weight).astype(jnp.bfloat16)
    d_mixed_heads = d_mixed.reshape(row_count, head_count, head_size).transpose(1, 0, 2)
    dot_terms = d_mixed.astype(jnp.float32) * mixed.astype(jnp.float32)
    row_dots = jnp.stack(
        [
            jnp.sum(dot_terms[:, h * head_size : (h + 1) * head_size], axis=-1, keepdims=True)
            for h in range(head_count)
        ]
    )

    def against(keys, values, probs):
        d_values = jnp.einsum(
            "hqk,hqd->kd", probs, d_mixed_heads, preferred_element_type=jnp.float32
        )
        d_probs = jnp.einsum(
            "hqd,kd->hqk", d_mixed_heads, values, preferred_element_type=jnp.float32
        )
        d_scores = (probs.astype(jnp.float32) * (d_probs - row_dots)).astype(jnp.bfloat16)
        d_keys = (
            jnp.einsum("hqk,hqd->kd", d_scores, query_heads, preferred_element_type=jnp.float32)
            * scale_factor
        )
        return (d_keys, d_values, d_scores)

    d_prior_keys, d_prior_values, d_prior_scores = against(prior_keys, prior_values, probs_prior)
    returned = from_behind(
        jnp.concatenate([d_prior_keys, d_prior_values], axis=1).astype(jnp.bfloat16), "fsdp", -1
    ).astype(jnp.float32)
    d_own_keys, d_own_values, d_own_scores = against(key_rot, value_proj, probs_own)
    d_query_heads = (
        jnp.einsum("hqk,kd->hqd", d_own_scores, key_rot, preferred_element_type=jnp.float32)
        + jnp.einsum("hqk,kd->hqd", d_prior_scores, prior_keys, preferred_element_type=jnp.float32)
    ) * scale_factor
    d_query_rows = d_query_heads.transpose(1, 0, 2)
    d_key_rot = d_own_keys + returned[:, :head_size]
    d_value = (d_own_values + returned[:, head_size:]).astype(jnp.bfloat16)

    def query_head(vector, gain_vec):
        return rotate(rms_scale(vector, gain_vec), cosine[:, None, :], sine_table[:, None, :])

    def key_head(vector, gain_vec):
        return rotate(rms_scale(vector, gain_vec), cosine, sine_table)

    d_query, grad_query_gain = pullback(query_head, query_proj, head_gain[0], d_query_rows)
    d_key, grad_key_gain = pullback(key_head, key_proj, head_gain[1], d_key_rot)
    d_query = d_query.reshape(row_count, query_width).astype(jnp.bfloat16)
    d_qkv = jnp.concatenate([d_query, d_key.astype(jnp.bfloat16), d_value], axis=1)
    grad_qkv = outer_dot(normed_in, d_qkv).astype(jnp.bfloat16)
    d_normed = dot_transposed(d_qkv, qkv_weight)
    d_input_part, grad_in_gain = pullback(rms_scale, inputs, norm_gain[0], d_normed)
    d_inputs = d_residual + d_input_part
    gain_grads = (grad_in_gain, grad_post_attn, grad_query_gain, grad_key_gain)
    return (d_inputs, (grad_qkv, grad_out_proj), gain_grads)


def with_gains(blocks, attn_gains, ff_gains):
    size = blocks.shape[0]
    norm_part = jnp.stack([attn_gains[0], attn_gains[1], ff_gains[0], ff_gains[1]])
    norm_part = norm_part.reshape(4, size, -1).transpose(1, 0, 2).reshape(size, -1)
    head_part = jnp.stack(attn_gains[2:]).reshape(2, size, -1).transpose(1, 0, 2).reshape(size, -1)
    row = jnp.concatenate([norm_part, head_part], axis=1).astype(blocks.dtype)
    row = jnp.pad(row[:, None, None], ((0, 0), (0, 0), (0, 15), (0, blocks.shape[3] - row.shape[1])))
    return jnp.concatenate([blocks, jnp.broadcast_to(row, (size, 2) + row.shape[2:])], axis=2)


def local(
    tokens,
    cotangent,
    lengths,
    query_weight,
    key_weight,
    value_weight,
    out_weight,
    gate_weight,
    up_weight,
    down_weight,
    norm_gains,
    head_gains,
):
    core = lax.axis_index("section")
    me = lax.axis_index("fsdp")
    first_core = core == 0
    row_count = tokens.shape[2]
    width = tokens.shape[3]
    query_width = query_weight.shape[2]
    head_size = key_weight.shape[2]
    qkv_width = query_width + 2 * head_size
    ff_width = gate_weight.shape[2]
    out_rows = out_weight.shape[1] // 2

    gain_count, gain_share = norm_gains.shape[1:]
    head_share = head_gains.shape[2]
    split_at = gain_count * gain_share
    gain_rows = jnp.stack(
        [
            norm_gains.reshape(split_at),
            jnp.pad(head_gains.reshape(-1), (0, split_at - 2 * head_share)),
        ]
    )
    gain_rows = jnp.pad(gain_rows, ((0, 14), (0, 0)))

    wide = jnp.concatenate(
        [query_weight[0], key_weight[0], value_weight[0], gate_weight[0], up_weight[0]], axis=1
    )
    wide = wide.reshape(2, -1, wide.shape[1])
    narrow = jnp.concatenate(
        [
            out_weight[0].reshape(2, -1, width),
            down_weight[0].reshape(2, -1, width),
            jnp.broadcast_to(gain_rows[None], (2,) + gain_rows.shape),
        ],
        axis=1,
    )
    layer_blocks = []
    for packed in (wide, narrow):
        arrived = swap_cores(lax.dynamic_index_in_dim(packed, 1 - core, 0, keepdims=False))
        kept = lax.dynamic_index_in_dim(packed, core, 0, keepdims=False)
        layer_blocks.append(
            (jnp.where(first_core, kept, arrived), jnp.where(first_core, arrived, kept))
        )

    def assemble(near_pair):
        wide_held, narrow_held = (gather_rows(pieces) for pieces in near_pair)
        wide_pair = (wide_held, swap_cores(wide_held))
        narrow_pair = (narrow_held, swap_cores(narrow_held))
        everything = slice(None)
        narrow_out = tuple(piece[:, :out_rows] for piece in narrow_pair)
        narrow_down = tuple(
            piece[:, out_rows : piece.shape[1] - gain_rows.shape[0]] for piece in narrow_pair
        )
        held_gains = narrow_held[:, narrow_held.shape[1] - gain_rows.shape[0] :]
        size = held_gains.shape[0]
        norm_gain = held_gains[:, 0].reshape(size, gain_count, gain_share)
        head_gain = held_gains[:, 1, : 2 * head_share].reshape(size, 2, head_share)
        return (
            join_rows(wide_pair, slice(0, qkv_width)),
            join_rows(narrow_out, everything),
            join_rows(wide_pair, slice(qkv_width, None)),
            join_rows(narrow_down, everything),
            norm_gain.transpose(1, 0, 2).reshape(gain_count, -1).astype(jnp.float32),
            head_gain.transpose(1, 0, 2).reshape(2, -1).astype(jnp.float32),
        )

    lower_near = [near_rows(blocks[0]) for blocks in layer_blocks]
    lower_near, upper_blocks = lax.optimization_barrier(
        (lower_near, [blocks[1] for blocks in layer_blocks])
    )
    upper_near = [near_rows(block) for block in upper_blocks]
    lower_params = assemble(lower_near)

    def own_micro(rows):
        return lax.dynamic_index_in_dim(rows, core, 0, keepdims=False)[0]

    doc_lengths = own_micro(lengths)
    places = me * row_count + jnp.arange(row_count, dtype=jnp.int32)
    prior_places = places - row_count
    doc_ids, offset = doc_layout(doc_lengths, places)
    prior_docs, unused = doc_layout(doc_lengths, prior_places)
    layout = (
        window_mask(doc_ids, places, doc_ids, places),
        window_mask(doc_ids, places, prior_docs, prior_places),
    ) + angle_tables(offset, head_size)

    lower_out, lower_state, upper_near = layer_forward(
        own_micro(tokens).astype(jnp.float32), lower_params, layout, upper_near
    )
    upper_params = assemble(upper_near)
    lower_out = lower_out.astype(jnp.bfloat16)
    upper_out, upper_state, unused = layer_forward(
        lower_out.astype(jnp.float32), upper_params, layout, ()
    )
    upper_out = upper_out.astype(jnp.bfloat16)

    d_residual, upper_ff, upper_ff_gains = ff_backward(
        own_micro(cotangent).astype(jnp.float32), upper_state, upper_params
    )
    upper_ff = [add_near(add_cores(row_blocks(grad))) for grad in upper_ff]
    d_middle, upper_attn, upper_attn_gains = attn_backward(
        d_residual, upper_state, upper_params, layout
    )
    upper_attn = [
        with_gains(row_blocks(upper_attn[0]), upper_attn_gains, upper_ff_gains),
        row_blocks(upper_attn[1]),
    ]
    d_middle, upper_ff = lax.optimization_barrier((d_middle, upper_ff))
    upper_ff = [add_far(pair) for pair in upper_ff]
    upper_attn = [add_near(add_cores(blocks)) for blocks in upper_attn]
    d_residual, lower_ff, lower_ff_gains = ff_backward(
        d_middle.astype(jnp.bfloat16).astype(jnp.float32), lower_state, lower_params
    )
    d_residual, upper_ff, upper_attn = lax.optimization_barrier(
        (d_residual, upper_ff, upper_attn)
    )
    upper_ff = [lax.psum(total, "rep") for total in upper_ff]
    upper_attn = [add_far(pair) for pair in upper_attn]
    lower_ff = [add_near(add_cores(row_blocks(grad))) for grad in lower_ff]
    d_tokens, lower_attn, lower_attn_gains = attn_backward(
        d_residual, lower_state, lower_params, layout
    )
    lower_attn = [
        with_gains(row_blocks(lower_attn[0]), lower_attn_gains, lower_ff_gains),
        row_blocks(lower_attn[1]),
    ]
    d_tokens, lower_attn, lower_ff, upper_attn = lax.optimization_barrier(
        (d_tokens, lower_attn, lower_ff, upper_attn)
    )
    lower_ff = [add_far(pair) for pair in lower_ff]
    upper_ff, rest = lax.optimization_barrier((upper_ff, upper_attn + lower_ff))
    rest = [lax.psum(total, "rep") for total in rest]
    lower_attn = [add_far(add_near(add_cores(blocks))) for blocks in lower_attn]
    rest, lower_attn = lax.optimization_barrier((rest, lower_attn))
    lower_attn = [lax.psum(total, "rep") for total in lower_attn]
    upper_sums = rest[:2] + upper_ff
    lower_sums = lower_attn + rest[2:]

    def for_layers(lower_value, upper_value):
        mine = jnp.where(first_core, lower_value, upper_value)
        theirs = jnp.where(first_core, upper_value, lower_value)
        return (mine, swap_cores(theirs.astype(jnp.bfloat16)).astype(mine.dtype))

    section_out = ordered(*(rows[None] for rows in for_layers(lower_out, upper_out)), 0)
    input_grad = ordered(*(rows[None] for rows in for_layers(d_tokens, d_middle)), 0)
    pairs = [
        for_layers(lower_sum, upper_sum) for lower_sum, upper_sum in zip(lower_sums, upper_sums)
    ]
    gain_sums = pairs[0][0][-16].astype(jnp.float32)
    norm_sums = gain_sums[:split_at].reshape(1, gain_count, gain_share)
    head_sums = gain_sums[split_at : split_at + 2 * head_share].reshape(1, 2, head_share)
    pairs[0] = tuple(piece[:-16] for piece in pairs[0])
    shares = [ordered(*pair, 0).astype(jnp.float32)[None] for pair in pairs]
    qkv_share, out_share, gate_up_share, down_share = shares
    return (
        section_out[None, :, None],
        input_grad[None, :, None],
        qkv_share[:, :, :query_width],
        qkv_share[:, :, query_width : query_width + head_size],
        qkv_share[:, :, query_width + head_size :],
        out_share,
        gate_up_share[:, :, :ff_width],
        gate_up_share[:, :, ff_width:],
        down_share,
        norm_sums,
        head_sums,
    )


def solution(mesh):
    return jax.shard_map(
        local,
        mesh=mesh,
        in_specs=(
            P(None, "rep", "fsdp", None),
            P(None, "rep", "fsdp", None),
            P(None, "rep", None),
            P("section", "fsdp", None),
            P("section", "fsdp", None),
            P("section", "fsdp", None),
            P("section", "fsdp", None),
            P("section", "fsdp", None),
            P("section", "fsdp", None),
            P("section", "fsdp", None),
            P("section", None, "fsdp"),
            P("section", None, "fsdp"),
        ),
        out_specs=(
            P("section", None, "rep", "fsdp", None),
            P("section", None, "rep", "fsdp", None),
            P("section", "fsdp", None),
            P("section", "fsdp", None),
            P("section", "fsdp", None),
            P("section", "fsdp", None),
            P("section", "fsdp", None),
            P("section", "fsdp", None),
            P("section", "fsdp", None),
            P("section", None, "fsdp"),
            P("section", None, "fsdp"),
        ),
        check_vma=False,
    )
```

```python
import math

import jax
import jax.numpy as jnp
from jax import lax
from jax.sharding import PartitionSpec as P

WINDOW = 512


epsilon = 1e-06
rope_base = 10000.0
neg_fill = -1e30
gelu_coef = 0.7978845608028654


def from_behind(block, axis, distance):
    devices = range(lax.axis_size(axis))
    route = [(i - distance, i) for i in devices if i - distance in devices]
    return lax.ppermute(block, axis, route)


def rms_scale(vector, gain_vec):
    return (
        vector * lax.rsqrt(jnp.mean(vector * vector, axis=-1, keepdims=True) + epsilon) * gain_vec
    )


def gelu_tanh(vector):
    return (
        0.5 * vector * (1.0 + jnp.tanh(gelu_coef * (vector + 0.044715 * vector * vector * vector)))
    )


def geglu(gate_proj, up_proj):
    return gelu_tanh(gate_proj) * up_proj


def rotate(vector, cosine, sine_table):
    half_width = vector.shape[-1] // 2
    first_half = vector[..., :half_width]
    second_half = vector[..., half_width:]
    return jnp.concatenate(
        [
            first_half * cosine - second_half * sine_table,
            second_half * cosine + first_half * sine_table,
        ],
        axis=-1,
    )


def angle_tables(offset, width):
    frequency = jnp.exp(
        jnp.arange(width // 2, dtype=jnp.float32) * (-2.0 * math.log(rope_base) / width)
    )
    angles = offset.astype(jnp.float32)[:, None] * frequency[None, :]
    return (jnp.cos(angles), jnp.sin(angles))


def doc_layout(doc_lengths, places):
    doc_ends = jnp.cumsum(doc_lengths)
    starts = doc_ends - doc_lengths
    doc_ids = jnp.sum((places[:, None] >= doc_ends[None, :]).astype(jnp.int32), axis=1)
    numbers = jnp.arange(doc_lengths.shape[0], dtype=jnp.int32)
    first_place = jnp.sum(
        jnp.where(doc_ids[:, None] == numbers[None, :], starts[None, :], 0), axis=1
    )
    return (doc_ids, places - first_place)


def window_mask(query_docs, query_places, key_docs, key_places):
    gap_rows = query_places[:, None] - key_places[None, :]
    same_doc = query_docs[:, None] == key_docs[None, :]
    return same_doc & (key_places[None, :] >= 0) & (gap_rows >= 0) & (gap_rows < WINDOW)


def outer_dot(left, right):
    return lax.dot_general(
        left, right, (((0,), (0,)), ((), ())), preferred_element_type=jnp.float32
    )


def dot_transposed(left, right):
    return lax.dot_general(
        left, right, (((1,), (1,)), ((), ())), preferred_element_type=jnp.float32
    )


def pullback(function, first_arg, second_arg, grad_value):
    unused, back = jax.vjp(function, first_arg, second_arg)
    return back(grad_value)


def block_scores(query_heads, key_block, allowed, scale_factor):
    raw_scores = (
        jnp.einsum("hqd,kd->hqk", query_heads, key_block, preferred_element_type=jnp.float32)
        * scale_factor
    )
    return jnp.where(allowed[None], raw_scores, neg_fill)


def bit_pair():
    second_core = lax.axis_index("section") == 1
    first_bit = jnp.where(second_core, 2, 1)
    return (first_bit, 3 - first_bit)


def hop(block, stage):
    size = lax.axis_size("fsdp")
    route = []
    for core in range(2):
        bit = 1 if core == stage else 2
        for place in range(size):
            route.append((core * size + place, core * size + (place ^ bit)))
    return lax.ppermute(block, ("section", "fsdp"), route)


def swap_cores(block):
    return lax.ppermute(block, "section", [(0, 1), (1, 0)])


def ordered(mine, other, axis):
    first_core = lax.axis_index("section") == 0
    return jnp.concatenate(
        [jnp.where(first_core, mine, other), jnp.where(first_core, other, mine)], axis=axis
    )


def near_rows(block):
    return (block, hop(block, 0), hop(block, 1))


def gather_rows(pieces):
    block, near, side = pieces
    me = lax.axis_index("fsdp")
    first_bit, second_bit = bit_pair()
    far = hop(near, 1)
    held = jnp.zeros((lax.axis_size("fsdp"),) + block.shape, block.dtype)
    for piece, place in (
        (block, me),
        (near, me ^ first_bit),
        (side, me ^ second_bit),
        (far, me ^ 3),
    ):
        held = lax.dynamic_update_index_in_dim(held, piece, place, 0)
    return held


def join_rows(pair, columns):
    mine, other = pair
    mine = mine[:, None, :, columns]
    other = other[:, None, :, columns]
    whole = ordered(mine, other, 1)
    return whole.reshape(-1, whole.shape[-1])


def pick(source, place):
    return lax.dynamic_index_in_dim(source, place, 0, keepdims=False)


def row_blocks(grad):
    size = lax.axis_size("fsdp")
    return grad.reshape(size, 2, grad.shape[0] // (2 * size), grad.shape[1])


def add_cores(blocks):
    core = lax.axis_index("section")
    arrived = swap_cores(lax.dynamic_index_in_dim(blocks, 1 - core, 1, keepdims=False))
    kept = lax.dynamic_index_in_dim(blocks, core, 1, keepdims=False)
    return kept.astype(jnp.float32) + arrived.astype(jnp.float32)


def add_near(total):
    me = lax.axis_index("fsdp")
    first_bit, second_bit = bit_pair()
    near = hop(
        jnp.stack([pick(total, me ^ first_bit), pick(total, me ^ 3)]).astype(jnp.bfloat16), 0
    ).astype(jnp.float32)
    return (
        pick(total, me) + near[0],
        (pick(total, me ^ second_bit) + near[1]).astype(jnp.bfloat16),
    )


def add_far(pair):
    return (pair[0] + hop(pair[1], 1).astype(jnp.float32)).astype(jnp.bfloat16)


def layer_forward(inputs, params, layout, pending):
    qkv_weight, out_weight, gu_weight, down_weight, norm_gain, head_gain = params
    allowed_own, allowed_prior, cosine, sine_table = layout
    row_count = inputs.shape[0]
    head_size = head_gain.shape[1]
    query_width = out_weight.shape[0]
    head_count = query_width // head_size
    ff_width = down_weight.shape[0]
    scale_factor = head_size ** (-0.5)
    normed_in = rms_scale(inputs, norm_gain[0]).astype(jnp.bfloat16)
    kv_proj = jnp.dot(
        normed_in, qkv_weight[:, query_width:], preferred_element_type=jnp.float32
    )
    key_proj = kv_proj[:, :head_size]
    value_proj = kv_proj[:, head_size:].astype(jnp.bfloat16)
    key_rot = rotate(rms_scale(key_proj, head_gain[1]), cosine, sine_table).astype(jnp.bfloat16)
    prior_rows = from_behind(jnp.concatenate([key_rot, value_proj], axis=1), "fsdp", 1)
    query_proj = jnp.dot(
        normed_in, qkv_weight[:, :query_width], preferred_element_type=jnp.float32
    ).reshape(row_count, head_count, head_size)
    query_rot = rotate(
        rms_scale(query_proj, head_gain[0]), cosine[:, None, :], sine_table[:, None, :]
    ).astype(jnp.bfloat16)
    prior_keys = prior_rows[:, :head_size]
    prior_values = prior_rows[:, head_size:]
    query_heads = query_rot.transpose(1, 0, 2)
    scores_own = block_scores(query_heads, key_rot, allowed_own, scale_factor)
    scores_prior = block_scores(query_heads, prior_keys, allowed_prior, scale_factor)
    row_max = jnp.maximum(
        jnp.max(scores_own, axis=-1, keepdims=True), jnp.max(scores_prior, axis=-1, keepdims=True)
    )
    exp_own = jnp.exp(scores_own - row_max)
    exp_prior = jnp.exp(scores_prior - row_max)
    inverse = 1.0 / (
        jnp.sum(exp_own, axis=-1, keepdims=True) + jnp.sum(exp_prior, axis=-1, keepdims=True)
    )
    probs_own = (exp_own * inverse).astype(jnp.bfloat16)
    probs_prior = (exp_prior * inverse).astype(jnp.bfloat16)
    mixed_heads = jnp.einsum(
        "hqk,kd->hqd", probs_own, value_proj, preferred_element_type=jnp.float32
    ) + jnp.einsum("hqk,kd->hqd", probs_prior, prior_values, preferred_element_type=jnp.float32)
    mixed = mixed_heads.transpose(1, 0, 2).reshape(row_count, query_width).astype(jnp.bfloat16)
    attn_proj = jnp.dot(mixed, out_weight, preferred_element_type=jnp.float32)
    residual = inputs + rms_scale(attn_proj, norm_gain[1])
    residual, pending = lax.optimization_barrier((residual, pending))
    ff_in = rms_scale(residual, norm_gain[2]).astype(jnp.bfloat16)
    gate_proj = jnp.dot(ff_in, gu_weight[:, :ff_width], preferred_element_type=jnp.float32)
    up_proj = jnp.dot(ff_in, gu_weight[:, ff_width:], preferred_element_type=jnp.float32)
    hidden = geglu(gate_proj, up_proj).astype(jnp.bfloat16)
    ff_out = jnp.dot(hidden, down_weight, preferred_element_type=jnp.float32)
    outputs = residual + rms_scale(ff_out, norm_gain[3])
    kept_state = (
        inputs,
        normed_in,
        query_proj,
        key_proj,
        query_heads,
        key_rot,
        value_proj,
        prior_keys,
        prior_values,
        probs_own,
        probs_prior,
        mixed,
        attn_proj,
        residual,
        ff_in,
        gate_proj,
        up_proj,
        hidden,
        ff_out,
    )
    return (outputs, kept_state, pending)


def ff_backward(grad_out, kept_state, params):
    qkv_weight, out_weight, gu_weight, down_weight, norm_gain, head_gain = params
    (
        inputs,
        normed_in,
        query_proj,
        key_proj,
        query_heads,
        key_rot,
        value_proj,
        prior_keys,
        prior_values,
        probs_own,
        probs_prior,
        mixed,
        attn_proj,
        residual,
        ff_in,
        gate_proj,
        up_proj,
        hidden,
        ff_out,
    ) = kept_state
    d_ff_out, grad_post_ff = pullback(rms_scale, ff_out, norm_gain[3], grad_out)
    d_ff_out = d_ff_out.astype(jnp.bfloat16)
    grad_down = outer_dot(hidden, d_ff_out).astype(jnp.bfloat16)
    d_hidden = dot_transposed(d_ff_out, down_weight).astype(jnp.bfloat16)
    d_gate, d_up = pullback(geglu, gate_proj, up_proj, d_hidden.astype(jnp.float32))
    d_gate_up = jnp.concatenate([d_gate.astype(jnp.bfloat16), d_up.astype(jnp.bfloat16)], axis=1)
    grad_gate_up = outer_dot(ff_in, d_gate_up).astype(jnp.bfloat16)
    d_ff_in = dot_transposed(d_gate_up, gu_weight)
    d_resid_part, grad_pre_ff = pullback(rms_scale, residual, norm_gain[2], d_ff_in)
    d_residual = grad_out + d_resid_part
    return (d_residual, (grad_gate_up, grad_down), (grad_pre_ff, grad_post_ff))


def attn_backward(d_residual, kept_state, params, layout):
    qkv_weight, out_weight, gu_weight, down_weight, norm_gain, head_gain = params
    unused_own, unused_prior, cosine, sine_table = layout
    (
        inputs,
        normed_in,
        query_proj,
        key_proj,
        query_heads,
        key_rot,
        value_proj,
        prior_keys,
        prior_values,
        probs_own,
        probs_prior,
        mixed,
        attn_proj,
        residual,
        ff_in,
        gate_proj,
        up_proj,
        hidden,
        ff_out,
    ) = kept_state
    row_count = inputs.shape[0]
    head_size = head_gain.shape[1]
    query_width = out_weight.shape[0]
    head_count = query_width // head_size
    scale_factor = head_size ** (-0.5)
    d_attn, grad_post_attn = pullback(rms_scale, attn_proj, norm_gain[1], d_residual)
    d_attn = d_attn.astype(jnp.bfloat16)
    grad_out_proj = outer_dot(mixed, d_attn).astype(jnp.bfloat16)
    d_mixed = dot_transposed(d_attn, out_weight).astype(jnp.bfloat16)
    d_mixed_heads = d_mixed.reshape(row_count, head_count, head_size).transpose(1, 0, 2)
    dot_terms = d_mixed.astype(jnp.float32) * mixed.astype(jnp.float32)
    row_dots = jnp.stack(
        [
            jnp.sum(dot_terms[:, h * head_size : (h + 1) * head_size], axis=-1, keepdims=True)
            for h in range(head_count)
        ]
    )

    def against(keys, values, probs):
        d_values = jnp.einsum(
            "hqk,hqd->kd", probs, d_mixed_heads, preferred_element_type=jnp.float32
        )
        d_probs = jnp.einsum(
            "hqd,kd->hqk", d_mixed_heads, values, preferred_element_type=jnp.float32
        )
        d_scores = (probs.astype(jnp.float32) * (d_probs - row_dots)).astype(jnp.bfloat16)
        d_keys = (
            jnp.einsum("hqk,hqd->kd", d_scores, query_heads, preferred_element_type=jnp.float32)
            * scale_factor
        )
        return (d_keys, d_values, d_scores)

    d_prior_keys, d_prior_values, d_prior_scores = against(prior_keys, prior_values, probs_prior)
    returned = from_behind(
        jnp.concatenate([d_prior_keys, d_prior_values], axis=1).astype(jnp.bfloat16), "fsdp", -1
    ).astype(jnp.float32)
    d_own_keys, d_own_values, d_own_scores = against(key_rot, value_proj, probs_own)
    d_query_heads = (
        jnp.einsum("hqk,kd->hqd", d_own_scores, key_rot, preferred_element_type=jnp.float32)
        + jnp.einsum("hqk,kd->hqd", d_prior_scores, prior_keys, preferred_element_type=jnp.float32)
    ) * scale_factor
    d_query_rows = d_query_heads.transpose(1, 0, 2)
    d_key_rot = d_own_keys + returned[:, :head_size]
    d_value = (d_own_values + returned[:, head_size:]).astype(jnp.bfloat16)

    def query_head(vector, gain_vec):
        return rotate(rms_scale(vector, gain_vec), cosine[:, None, :], sine_table[:, None, :])

    def key_head(vector, gain_vec):
        return rotate(rms_scale(vector, gain_vec), cosine, sine_table)

    d_query, grad_query_gain = pullback(query_head, query_proj, head_gain[0], d_query_rows)
    d_key, grad_key_gain = pullback(key_head, key_proj, head_gain[1], d_key_rot)
    d_query = d_query.reshape(row_count, query_width).astype(jnp.bfloat16)
    d_qkv = jnp.concatenate([d_query, d_key.astype(jnp.bfloat16), d_value], axis=1)
    grad_qkv = outer_dot(normed_in, d_qkv).astype(jnp.bfloat16)
    d_normed = dot_transposed(d_qkv, qkv_weight)
    d_input_part, grad_in_gain = pullback(rms_scale, inputs, norm_gain[0], d_normed)
    d_inputs = d_residual + d_input_part
    gain_grads = (grad_in_gain, grad_post_attn, grad_query_gain, grad_key_gain)
    return (d_inputs, (grad_qkv, grad_out_proj), gain_grads)


def with_gains(blocks, attn_gains, ff_gains):
    size = blocks.shape[0]
    norm_part = jnp.stack([attn_gains[0], attn_gains[1], ff_gains[0], ff_gains[1]])
    norm_part = norm_part.reshape(4, size, -1).transpose(1, 0, 2).reshape(size, -1)
    head_part = jnp.stack(attn_gains[2:]).reshape(2, size, -1).transpose(1, 0, 2).reshape(size, -1)
    row = jnp.concatenate([norm_part, head_part], axis=1).astype(blocks.dtype)
    row = jnp.pad(row[:, None, None], ((0, 0), (0, 0), (0, 15), (0, blocks.shape[3] - row.shape[1])))
    return jnp.concatenate([blocks, jnp.broadcast_to(row, (size, 2) + row.shape[2:])], axis=2)


def local(
    tokens,
    cotangent,
    lengths,
    query_weight,
    key_weight,
    value_weight,
    out_weight,
    gate_weight,
    up_weight,
    down_weight,
    norm_gains,
    head_gains,
):
    core = lax.axis_index("section")
    me = lax.axis_index("fsdp")
    first_core = core == 0
    row_count = tokens.shape[2]
    width = tokens.shape[3]
    query_width = query_weight.shape[2]
    head_size = key_weight.shape[2]
    qkv_width = query_width + 2 * head_size
    ff_width = gate_weight.shape[2]
    out_rows = out_weight.shape[1] // 2

    gain_count, gain_share = norm_gains.shape[1:]
    head_share = head_gains.shape[2]
    split_at = gain_count * gain_share
    gain_rows = jnp.stack(
        [
            norm_gains.reshape(split_at),
            jnp.pad(head_gains.reshape(-1), (0, split_at - 2 * head_share)),
        ]
    )
    gain_rows = jnp.pad(gain_rows, ((0, 14), (0, 0)))

    wide = jnp.concatenate(
        [query_weight[0], key_weight[0], value_weight[0], gate_weight[0], up_weight[0]], axis=1
    )
    wide = wide.reshape(2, -1, wide.shape[1])
    narrow = jnp.concatenate(
        [
            out_weight[0].reshape(2, -1, width),
            down_weight[0].reshape(2, -1, width),
            jnp.broadcast_to(gain_rows[None], (2,) + gain_rows.shape),
        ],
        axis=1,
    )
    layer_blocks = []
    for packed in (wide, narrow):
        arrived = swap_cores(lax.dynamic_index_in_dim(packed, 1 - core, 0, keepdims=False))
        kept = lax.dynamic_index_in_dim(packed, core, 0, keepdims=False)
        layer_blocks.append(
            (jnp.where(first_core, kept, arrived), jnp.where(first_core, arrived, kept))
        )

    def assemble(near_pair):
        wide_held, narrow_held = (gather_rows(pieces) for pieces in near_pair)
        wide_pair = (wide_held, swap_cores(wide_held))
        narrow_pair = (narrow_held, swap_cores(narrow_held))
        everything = slice(None)
        narrow_out = tuple(piece[:, :out_rows] for piece in narrow_pair)
        narrow_down = tuple(
            piece[:, out_rows : piece.shape[1] - gain_rows.shape[0]] for piece in narrow_pair
        )
        held_gains = narrow_held[:, narrow_held.shape[1] - gain_rows.shape[0] :]
        size = held_gains.shape[0]
        norm_gain = held_gains[:, 0].reshape(size, gain_count, gain_share)
        head_gain = held_gains[:, 1, : 2 * head_share].reshape(size, 2, head_share)
        return (
            join_rows(wide_pair, slice(0, qkv_width)),
            join_rows(narrow_out, everything),
            join_rows(wide_pair, slice(qkv_width, None)),
            join_rows(narrow_down, everything),
            norm_gain.transpose(1, 0, 2).reshape(gain_count, -1).astype(jnp.float32),
            head_gain.transpose(1, 0, 2).reshape(2, -1).astype(jnp.float32),
        )

    lower_near = [near_rows(blocks[0]) for blocks in layer_blocks]
    lower_near, upper_blocks = lax.optimization_barrier(
        (lower_near, [blocks[1] for blocks in layer_blocks])
    )
    upper_near = [near_rows(block) for block in upper_blocks]
    lower_params = assemble(lower_near)

    def own_micro(rows):
        return lax.dynamic_index_in_dim(rows, core, 0, keepdims=False)[0]

    doc_lengths = own_micro(lengths)
    places = me * row_count + jnp.arange(row_count, dtype=jnp.int32)
    prior_places = places - row_count
    doc_ids, offset = doc_layout(doc_lengths, places)
    prior_docs, unused = doc_layout(doc_lengths, prior_places)
    layout = (
        window_mask(doc_ids, places, doc_ids, places),
        window_mask(doc_ids, places, prior_docs, prior_places),
    ) + angle_tables(offset, head_size)

    lower_out, lower_state, upper_near = layer_forward(
        own_micro(tokens).astype(jnp.float32), lower_params, layout, upper_near
    )
    upper_params = assemble(upper_near)
    lower_out = lower_out.astype(jnp.bfloat16)
    upper_out, upper_state, unused = layer_forward(
        lower_out.astype(jnp.float32), upper_params, layout, ()
    )
    upper_out = upper_out.astype(jnp.bfloat16)

    d_residual, upper_ff, upper_ff_gains = ff_backward(
        own_micro(cotangent).astype(jnp.float32), upper_state, upper_params
    )
    upper_ff = [add_near(add_cores(row_blocks(grad))) for grad in upper_ff]
    d_middle, upper_attn, upper_attn_gains = attn_backward(
        d_residual, upper_state, upper_params, layout
    )
    upper_attn = [
        with_gains(row_blocks(upper_attn[0]), upper_attn_gains, upper_ff_gains),
        row_blocks(upper_attn[1]),
    ]
    d_middle, upper_ff = lax.optimization_barrier((d_middle, upper_ff))
    upper_ff = [add_far(pair) for pair in upper_ff]
    upper_attn = [add_near(add_cores(blocks)) for blocks in upper_attn]
    d_residual, lower_ff, lower_ff_gains = ff_backward(
        d_middle.astype(jnp.bfloat16).astype(jnp.float32), lower_state, lower_params
    )
    d_residual, upper_ff, upper_attn = lax.optimization_barrier(
        (d_residual, upper_ff, upper_attn)
    )
    upper_attn = [add_far(pair) for pair in upper_attn]
    upper_sums = [lax.psum(total, "rep") for total in upper_attn + upper_ff]
    lower_ff = [add_near(add_cores(row_blocks(grad))) for grad in lower_ff]
    d_tokens, lower_attn, lower_attn_gains = attn_backward(
        d_residual, lower_state, lower_params, layout
    )
    lower_attn = [
        with_gains(row_blocks(lower_attn[0]), lower_attn_gains, lower_ff_gains),
        row_blocks(lower_attn[1]),
    ]
    lower_ff = [add_far(pair) for pair in lower_ff]
    lower_attn = [add_far(add_near(add_cores(blocks))) for blocks in lower_attn]
    upper_sums, lower_sums = lax.optimization_barrier((upper_sums, lower_attn + lower_ff))
    lower_sums = [lax.psum(total, "rep") for total in lower_sums]

    def for_layers(lower_value, upper_value):
        mine = jnp.where(first_core, lower_value, upper_value)
        theirs = jnp.where(first_core, upper_value, lower_value)
        return (mine, swap_cores(theirs.astype(jnp.bfloat16)).astype(mine.dtype))

    section_out = ordered(*(rows[None] for rows in for_layers(lower_out, upper_out)), 0)
    input_grad = ordered(*(rows[None] for rows in for_layers(d_tokens, d_middle)), 0)
    pairs = [
        for_layers(lower_sum, upper_sum) for lower_sum, upper_sum in zip(lower_sums, upper_sums)
    ]
    gain_sums = pairs[0][0][-16].astype(jnp.float32)
    norm_sums = gain_sums[:split_at].reshape(1, gain_count, gain_share)
    head_sums = gain_sums[split_at : split_at + 2 * head_share].reshape(1, 2, head_share)
    pairs[0] = tuple(piece[:-16] for piece in pairs[0])
    shares = [ordered(*pair, 0).astype(jnp.float32)[None] for pair in pairs]
    qkv_share, out_share, gate_up_share, down_share = shares
    return (
        section_out[None, :, None],
        input_grad[None, :, None],
        qkv_share[:, :, :query_width],
        qkv_share[:, :, query_width : query_width + head_size],
        qkv_share[:, :, query_width + head_size :],
        out_share,
        gate_up_share[:, :, :ff_width],
        gate_up_share[:, :, ff_width:],
        down_share,
        norm_sums,
        head_sums,
    )


def solution(mesh):
    return jax.shard_map(
        local,
        mesh=mesh,
        in_specs=(
            P(None, "rep", "fsdp", None),
            P(None, "rep", "fsdp", None),
            P(None, "rep", None),
            P("section", "fsdp", None),
            P("section", "fsdp", None),
            P("section", "fsdp", None),
            P("section", "fsdp", None),
            P("section", "fsdp", None),
            P("section", "fsdp", None),
            P("section", "fsdp", None),
            P("section", None, "fsdp"),
            P("section", None, "fsdp"),
        ),
        out_specs=(
            P("section", None, "rep", "fsdp", None),
            P("section", None, "rep", "fsdp", None),
            P("section", "fsdp", None),
            P("section", "fsdp", None),
            P("section", "fsdp", None),
            P("section", "fsdp", None),
            P("section", "fsdp", None),
            P("section", "fsdp", None),
            P("section", "fsdp", None),
            P("section", None, "fsdp"),
            P("section", None, "fsdp"),
        ),
        check_vma=False,
    )
```
